32 devices in a mesh: cd: 8 (over z, core), ij: 4 (over y, x).
Axes of the slice: x: 2, y: 2, z: 4, core: 2. Of those that a mesh axis runs over, the one named last changes fastest.
Arguments:
- left_factor: bfloat16 [4096, 4096], P('cd'), may hold values from -6 to 6
- right_factor: bfloat16 [4096, 4, 1024], P(None, None, 'ij'), may hold values from -0.09375 to 0.09375
- amplitudes: float32 [8, 192, 1024], P('ij', 'cd'), may hold values from -0.0390625 to 0.0390625
- heights: int32 [8], P('cd'), may hold values from 256 to 512, as said below
- owner_map: int32 [8, 512, 1], P('cd'), may hold values from 0 to 7; in each aligned block of 512 rows (0 to 511, 512 to 1023, ..., all dimensions but the last counted through in order) at most 96 rows name the same one
- row_site: int32 [8, 512], P('cd'), may hold values from 0 to 23
Outputs:
- residual: float32 [32], P(('ij', 'cd'))
The draws below stay inside these ranges and needn't reach their ends.
Inputs may be any that keep to these rules, and one draw needn't show every extreme that they name: `heights`: some former has exactly 512 live rows. `owner_map`: within the 512 rows of one former no tile is named more than 96 times, and that bound is reached.
All inputs are finite; a program needn't handle non-finite values.
Results may differ from the reference program's by a relative error of at most 0.0028.
Values may be sent and summed in bfloat16 or wider, within the bound.
A program may use at most 64 MiB of HBM per device.

```python
import math
import jax
import jax.numpy as jnp
import numpy as np
from jax import lax

NAUX = 4096
VIRT = 1024
NB = 4
C_TILE = 24
HMAX = 512
CAP = 96
NC = 192
NIJ = 8
FORMED = 4096
N_CD = 8


def draw_heights(key, part):
    first, second = jax.random.split(jax.random.fold_in(key, 11))
    drawn = jax.random.randint(first, (N_CD,), HMAX // 2, HMAX + 1)
    tallest = jax.random.randint(second, (), 0, N_CD)
    return jnp.where(jnp.arange(N_CD) == tallest, HMAX, drawn).astype(jnp.int32)


def with_ends(values, own_key, smallest, largest):
    longest = values.shape.index(max(values.shape))
    spots = []
    for shift in (0, 1):
        where = [jax.random.randint(jax.random.fold_in(own_key, axis), (), 0, length) for axis, length in enumerate(values.shape)]
        where[longest] = (where[longest] + shift) % values.shape[longest]
        spots.append(tuple(where))
    return values.at[spots[0]].set(smallest).at[spots[1]].set(largest)


def block_scale(key, shape, cuts, least, top_value):
    def one(axis_at, parts):
        draws = jax.random.uniform(jax.random.fold_in(jax.random.fold_in(key, 6), axis_at), (parts,), jnp.float32, least / len(cuts), top_value / len(cuts))
        return jnp.repeat(jnp.exp(draws), shape[axis_at] // parts).reshape((-1,) + (1,) * (len(shape) - axis_at - 1))

    gain = one(*cuts[0])
    for cut in cuts[1:]:
        gain = gain * one(*cut)
    return gain


def shared_out(stream_key, own, number, rows, amount, top, reach, slope):
    ranking = jax.random.permutation(stream_key, amount)
    heavy_load, usual = load_shares(amount, rows * top, reach, slope, True), load_shares(amount, rows * top, reach, slope, False)
    places = jnp.arange(amount)

    def named(lengths, turn):
        used = int((lengths > 0).sum())
        fixed = max(1, used // 4)
        passed = fixed + (places - fixed + turn * (used - fixed)) % max(1, amount - fixed)
        return jnp.zeros((amount,), jnp.int32).at[ranking[jnp.where(places < fixed, places, passed)]].set(jnp.asarray(lengths, jnp.int32))

    lengths = jnp.where(number % 4 == 0, named(heavy_load, number // 4), named(usual, number - number // 4 - 1))
    mixed = jax.random.permutation(jax.random.fold_in(own, 3), amount)
    giver, taker = mixed[0:amount // 2 * 2:2], mixed[1:amount // 2 * 2:2]
    room = jnp.minimum(lengths[giver] - 1, reach - lengths[taker]) // 2
    room = jnp.where((giver == ranking[0]) | (taker == ranking[0]) | (lengths[taker] == 0), 0, jnp.maximum(room, 0))
    passed = jax.random.randint(jax.random.fold_in(own, 4), (amount // 2,), 0, 1 << 20) % (room + 1)
    lengths = lengths.at[giver].add(-passed).at[taker].add(passed)
    members = jnp.searchsorted(jnp.cumsum(lengths), jnp.arange(rows * top), side="right").astype(jnp.int32)
    grid = members.reshape(top, rows).T
    grid = grid[jax.random.permutation(jax.random.fold_in(own, 1), rows)]
    turn = jax.random.randint(jax.random.fold_in(own, 2), (rows, 1), 0, top)
    return jnp.take_along_axis(grid, (jnp.arange(top)[None, :] + turn) % top, axis=1)


def load_shares(count, total, most, slope, full):
    portions = [(1 << 20) // math.isqrt(standing ** slope) + 1 for standing in range(1, count + 1)]
    largest = most if full else min(most, max(-(-total // count), total * portions[0] // sum(portions)))
    least = 1 if total - largest >= count - 1 else 0
    counts, rest = [largest] + [least] * (count - 1), total - largest - least * (count - 1)
    while rest > 0:
        free = [i for i in range(1, count) if counts[i] < largest] or [i for i in range(1, count) if counts[i] < most]
        mass, budget = sum([portions[i] for i in free]), rest
        for i in free:
            extra = min(most - counts[i], max(1, budget * portions[i] // mass), rest)
            counts[i] = counts[i] + extra
            rest = rest - extra
    return np.array(counts)


def normal_values(own_key, shape, deviation, most, cuts=(), kind=jnp.bfloat16):
    result = jax.random.normal(own_key, shape, jnp.float32) * deviation
    if len(cuts) > 0:
        result = block_scale(own_key, shape, cuts, -0.22, 0.18) * result
    return jnp.clip(result, min=-most, max=most).astype(kind)


def setup_inputs(seed: int = 0) -> dict:
    keys = jax.random.split(jax.random.key(seed), 7)
    left_factor = normal_values(keys[0], (FORMED, NAUX), 1.0, 6.0, ((0, 8),))
    right_factor = normal_values(keys[1], (NAUX, NB, VIRT), NAUX ** -0.5, 0.09375, ((2, 4),))
    amplitudes = normal_values(keys[2], (NIJ, NC, VIRT), (NC * VIRT // 8) ** -0.5, 0.0390625, ((0, 4), (1, 8)), jnp.float32)
    heights = draw_heights(jax.random.fold_in(keys[6], 71), 0)
    owner_map_keys = jax.random.split(jax.random.fold_in(keys[4], 1), N_CD * HMAX // HMAX)
    owner_map_turns = jax.random.permutation(jax.random.fold_in(keys[4], 3), N_CD * HMAX // HMAX)
    owner_map = jax.vmap(lambda own, number: shared_out(jax.random.fold_in(keys[4], 2), own, number, HMAX, N_CD, 1, CAP, 2))(owner_map_keys, owner_map_turns).reshape((N_CD, HMAX, 1))
    row_site = with_ends(jax.random.randint(keys[5], (N_CD, HMAX), 0, C_TILE), jax.random.fold_in(keys[5], 1), 0, C_TILE - 1).astype(jnp.int32)
    return dict(left_factor=left_factor, right_factor=right_factor, amplitudes=amplitudes, heights=heights, owner_map=owner_map, row_site=row_site)


def reference(left_factor, right_factor, amplitudes, heights, owner_map, row_site):
    formers = heights.shape[0]
    rows = left_factor.shape[0] // formers
    panel = jnp.dot(left_factor, right_factor.reshape(right_factor.shape[0], -1), preferred_element_type=jnp.float32)
    position = jnp.arange(rows, dtype=jnp.int32)
    live = (position[None, :] < heights[:, None]).reshape(-1)
    panel = jnp.where(live[:, None], panel, 0.0).astype(jnp.bfloat16).astype(jnp.float32)
    orbital = (owner_map[:, :, 0] * C_TILE + row_site).reshape(-1).astype(jnp.int32)
    sums = jax.ops.segment_sum(panel, orbital, num_segments=NC)
    sums = sums.reshape(NC, NB, VIRT)
    residual = jnp.einsum("icd,cbd->ib", amplitudes.astype(jnp.float32), sums, precision=lax.Precision.HIGHEST)
    return residual.reshape(-1)
```

```python
import functools

import jax
import jax.numpy as jnp
from jax import lax
from jax.experimental import pallas as pl
from jax.experimental.pallas import tpu as pltpu
from jax.sharding import PartitionSpec as P

LANES = 128
SIDE = 256
MESH = pl.DeviceIdType.MESH


def ladder_kernel(
    formers, blocks, nb, depth_chunks,
    amp_ref, label_ref, left_ref, right_ref, out_ref,
    left_v, right_v, sorted_v, first_panel, sums, pair_in, joined, tiles_in, amp_in, rows_out, rows_in,
    left_sem, right_sem, amp_send, amp_recv, pair_send, pair_recv,
    tile_send, tile_recv, row_send, row_recv,
):
    f = lax.axis_index("cd")
    j = lax.axis_index("ij")
    chips = formers // 2
    z = lax.div(f, 2)
    core = lax.rem(f, 2)
    devices = formers * blocks
    me = j * formers + f

    rows, depth = left_v.shape
    kc = depth // depth_chunks
    lane_tiles = right_v.shape[0] // (depth * nb)
    group = nb * lane_tiles
    per = SIDE // group
    dpiece = lane_tiles * LANES
    ni, tile, _ = amp_ref.shape

    def load(k):
        return (
            pltpu.make_async_copy(
                right_ref.at[pl.ds(k * kc * group, kc * group)],
                right_v.at[pl.ds(k * kc * group, kc * group)],
                right_sem.at[k],
            ),
            pltpu.make_async_copy(
                left_ref.at[:, pl.ds(k * kc, kc)],
                left_v.at[:, pl.ds(k * kc, kc)],
                left_sem.at[k],
            ),
        )

    def remote(src, dst, send, recv, to_f, to_j):
        return pltpu.make_async_remote_copy(
            src_ref=src, dst_ref=dst, send_sem=send, recv_sem=recv,
            device_id={"cd": to_f, "ij": to_j}, device_id_type=MESH,
        )

    def amp_copy(k, landing):
        to_j = lax.rem(j + k, blocks)
        slot = j if landing is None else to_j
        columns = pl.ds(pl.multiple_of(to_j * dpiece, dpiece), dpiece)
        return remote(
            amp_ref.at[:, :, columns], amp_in.at[slot],
            amp_send.at[to_j], amp_recv.at[slot], f, to_j,
        )

    def pair_copy(b):
        return remote(
            sums.at[b, 1 - core], pair_in.at[b], pair_send.at[b], pair_recv.at[b],
            f + 1 - 2 * core, j,
        )

    def tile_copy(b, k, landing):
        to_z = lax.rem(z + k, chips)
        slot = z if landing is None else to_z
        return remote(
            joined.at[b, to_z], tiles_in.at[b, slot],
            tile_send.at[b, to_z], tile_recv.at[b, slot], to_z * 2 + core, j,
        )

    def row_copy(k, landing):
        flat = lax.rem(me + k, devices)
        slot = me if landing is None else flat
        return remote(
            rows_out.at[flat], rows_in.at[slot], row_send.at[flat], row_recv.at[slot],
            lax.rem(flat, formers), lax.div(flat, formers),
        )

    for k in range(depth_chunks):
        for copy in load(k):
            copy.start()

    barrier = pltpu.get_barrier_semaphore()

    @pl.loop(1, devices)
    def _(k):
        flat = lax.rem(me + k, devices)
        pl.semaphore_signal(
            barrier, inc=1,
            device_id={"cd": lax.rem(flat, formers), "ij": lax.div(flat, formers)},
            device_id_type=MESH,
        )

    to = lax.broadcasted_iota(jnp.int32, (SIDE, SIDE), 0)
    origin = lax.broadcasted_iota(jnp.int32, (SIDE, SIDE), 1)
    reorder = (origin == (to % per) * group + to // per).astype(jnp.bfloat16)
    chosen = (
        lax.broadcasted_iota(jnp.int32, (formers * tile, rows), 0) == label_ref[...]
    ).astype(jnp.bfloat16)

    for k in range(depth_chunks):
        for copy in load(k):
            copy.wait()

        @pl.loop(0, kc // (2 * per))
        def _(m):
            base = pl.multiple_of(k * kc * group + m * (2 * SIDE), 2 * SIDE)
            both = jnp.concatenate(
                [right_v[pl.ds(base, SIDE), :], right_v[pl.ds(base + SIDE, SIDE), :]], axis=1
            )
            moved = jnp.dot(reorder, both, preferred_element_type=jnp.float32).astype(jnp.bfloat16)
            first = pl.multiple_of(k * kc + m * (2 * per), 2 * per)
            for g in range(group):
                column = (g // nb) * LANES
                piece = moved[g * per : (g + 1) * per]
                stacked = jnp.concatenate([piece[:, :LANES], piece[:, LANES:]], axis=0)
                sorted_v[g % nb, pl.ds(first, 2 * per), column : column + LANES] = stacked

        product = jnp.dot(
            left_v[:, k * kc : (k + 1) * kc],
            sorted_v[0, k * kc : (k + 1) * kc, :],
            preferred_element_type=jnp.float32,
        )
        if k == 0:
            first_panel[...] = product
            pl.semaphore_wait(barrier, devices - 1)
            for n in range(1, blocks):
                amp_copy(n, None).start()
        else:
            first_panel[...] = first_panel[...] + product

    def add_rows(b, panel):
        local = jnp.dot(chosen, panel.astype(jnp.bfloat16), preferred_element_type=jnp.float32)
        sums[b] = local.reshape(2, chips, tile, dpiece)
        pair_copy(b).start()

    def join(b):
        pair_copy(b).wait()
        joined[b] = sums[b, core] + pair_in[b]
        for n in range(1, chips):
            tile_copy(b, n, None).start()
        tiles_in[b, z] = joined[b, z]

    add_rows(0, first_panel[...])

    @pl.loop(1, nb)
    def _(b):
        panel = jnp.dot(left_v[...], sorted_v[b], preferred_element_type=jnp.float32)
        join(b - 1)
        add_rows(b, panel)

    for n in range(1, blocks):
        amp_copy(n, True).wait()
    amp_in[j] = amp_ref[:, :, pl.ds(pl.multiple_of(j * dpiece, dpiece), dpiece)]
    join(nb - 1)

    def fold(x):
        parts = [
            x[r : r + 8, c : c + LANES]
            for r in range(0, tile, 8)
            for c in range(0, dpiece, LANES)
        ]
        return functools.reduce(jnp.add, parts)

    for b in range(nb):
        for n in range(1, chips):
            tile_copy(b, n, True).wait()
        whole = tiles_in[b, 0]
        for n in range(1, chips):
            whole = whole + tiles_in[b, n]
        for s in range(blocks):
            for i in range(ni):
                rows_out[(s * ni + i) * nb + b] = jnp.sum(
                    fold(amp_in[s, i] * whole), axis=0, keepdims=True
                )

    @pl.loop(1, devices)
    def _(k):
        row_copy(k, None).start()

    rows_in[me] = rows_out[me]

    @pl.loop(1, devices)
    def _(k):
        row_copy(k, True).wait()

    total = rows_in[0]
    for s in range(1, devices):
        total = total + rows_in[s]
    out_ref[...] = jnp.sum(total, axis=1, keepdims=True)


def fits(left_factor, right_factor, amplitudes, formers, blocks):
    depth, nb, dpiece = right_factor.shape
    ni, tile, _ = amplitudes.shape
    if dpiece % LANES or tile % 8 or left_factor.shape[0] % 16 or formers % 2:
        return False
    group = nb * (dpiece // LANES)
    if SIDE % group or (SIDE // group) % 16 or nb < 2:
        return False
    if depth % (4 * SIDE) or ni * nb != formers:
        return False
    weights = 4 * depth * nb * dpiece + 2 * left_factor.size
    held = 4 * formers * tile * nb * dpiece * 3
    return held + weights < (40 << 20)


def by_kernel(left_factor, right_factor, amplitudes, heights, owner_map, row_site):
    formers = lax.axis_size("cd")
    blocks = lax.axis_size("ij")
    devices = formers * blocks
    chips = formers // 2
    rows, depth = left_factor.shape
    _, nb, dpiece = right_factor.shape
    ni, tile, _ = amplitudes.shape
    lane_tiles = dpiece // LANES
    chunks = 4
    live = jnp.arange(rows, dtype=jnp.int32)[None, :] < heights[0]
    owner = owner_map[:, :, 0]
    label = jnp.where(live, ((owner % 2) * chips + owner // 2) * tile + row_site, -1)
    flat_right = (
        right_factor.reshape(depth, nb, lane_tiles, LANES)
        .transpose(0, 2, 1, 3)
        .reshape(depth * lane_tiles * nb, LANES)
    )
    vmem = pl.BlockSpec(memory_space=pltpu.VMEM)
    hbm = pl.BlockSpec(memory_space=pl.ANY)
    dma = pltpu.SemaphoreType.DMA
    value = pl.pallas_call(
        functools.partial(ladder_kernel, formers, blocks, nb, chunks),
        out_shape=jax.ShapeDtypeStruct((1, 1), jnp.float32),
        in_specs=[vmem, vmem, hbm, hbm],
        out_specs=vmem,
        scratch_shapes=[
            pltpu.VMEM((rows, depth), jnp.bfloat16),
            pltpu.VMEM((depth * lane_tiles * nb, LANES), jnp.bfloat16),
            pltpu.VMEM((nb, depth, dpiece), jnp.bfloat16),
            pltpu.VMEM((rows, dpiece), jnp.float32),
            pltpu.VMEM((nb, 2, chips, tile, dpiece), jnp.float32),
            pltpu.VMEM((nb, chips, tile, dpiece), jnp.float32),
            pltpu.VMEM((nb, chips, tile, dpiece), jnp.float32),
            pltpu.VMEM((nb, chips, tile, dpiece), jnp.float32),
            pltpu.VMEM((blocks, ni, tile, dpiece), jnp.float32),
            pltpu.VMEM((devices, 1, LANES), jnp.float32),
            pltpu.VMEM((devices, 1, LANES), jnp.float32),
            dma((chunks,)),
            dma((chunks,)),
            dma((blocks,)),
            dma((blocks,)),
            dma((nb,)),
            dma((nb,)),
            dma((nb, chips)),
            dma((nb, chips)),
            dma((devices,)),
            dma((devices,)),
        ],
        compiler_params=pltpu.CompilerParams(
            collective_id=0, has_side_effects=True, vmem_limit_bytes=56 << 20
        ),
    )(amplitudes, label, left_factor, flat_right)
    return value.reshape(1)


def contract(amplitudes, sums):
    return jnp.einsum("icd,cbd->ib", amplitudes, sums, precision=lax.Precision.HIGHEST)


def by_rows(left_factor, right_factor, amplitudes, heights, owner_map, row_site):
    rows = left_factor.shape[0]
    formers = lax.axis_size("cd")
    capacity = (rows + formers - 1) // formers + rows // (2 * formers)
    bwidth = right_factor.shape[1]
    dpiece = right_factor.shape[2]
    tile = amplitudes.shape[1]
    panel = jnp.dot(
        left_factor,
        right_factor.reshape(right_factor.shape[0], -1),
        preferred_element_type=jnp.float32,
    )
    position = jnp.arange(rows, dtype=jnp.int32)
    live = position < heights[0]
    panel = jnp.where(live[:, None], panel, 0.0).astype(jnp.bfloat16)
    owners = owner_map[0, :, 0]
    hits = (owners[:, None] == jnp.arange(formers, dtype=jnp.int32)[None, :]) & live[:, None]
    places = jnp.cumsum(hits.astype(jnp.int32), axis=0) - 1
    within = jnp.sum(jnp.where(hits, places, 0), axis=1)
    target = jnp.where(live, owners * capacity + within, -1)
    dispatch = jnp.arange(formers * capacity, dtype=jnp.int32)[:, None] == target[None, :]
    outgoing = jnp.dot(
        dispatch.astype(jnp.bfloat16), panel, preferred_element_type=jnp.float32
    ).astype(jnp.bfloat16)
    labels = jnp.dot(dispatch.astype(jnp.float32), row_site[0].astype(jnp.float32)).astype(
        jnp.int32
    )
    outgoing = outgoing.reshape(formers, capacity, bwidth, dpiece)
    labels = labels.reshape(formers, capacity)
    arrived, arrived_labels = (
        lax.all_to_all(outgoing, "cd", split_axis=0, concat_axis=0, tiled=True),
        lax.all_to_all(labels, "cd", split_axis=0, concat_axis=0, tiled=True),
    )
    arrived = arrived.reshape(formers * capacity, bwidth, dpiece)
    picker = (
        jnp.arange(tile, dtype=jnp.int32)[:, None] == arrived_labels.reshape(-1)[None, :]
    ).astype(jnp.bfloat16)
    whole = lax.all_gather(
        jnp.einsum("cr,rbd->cbd", picker, arrived, preferred_element_type=jnp.float32),
        "ij",
        axis=2,
        tiled=True,
    )
    partial_value = contract(amplitudes, whole)
    return lax.psum_scatter(partial_value.reshape(-1), "cd", scatter_dimension=0, tiled=True)


def on_device(left_factor, right_factor, amplitudes, heights, owner_map, row_site):
    args = (left_factor, right_factor, amplitudes, heights, owner_map, row_site)
    sizes = lax.axis_size("cd"), lax.axis_size("ij")
    if fits(left_factor, right_factor, amplitudes, *sizes):
        return by_kernel(*args)
    return by_rows(*args)


def solution(mesh):
    placed = (
        P("cd", None),
        P(None, None, "ij"),
        P("ij", "cd", None),
        P("cd"),
        P("cd", None, None),
        P("cd", None),
    )
    return jax.shard_map(
        on_device, mesh=mesh, in_specs=placed, out_specs=P(("ij", "cd")), check_vma=False
    )
```

```python
import functools

import jax
import jax.numpy as jnp
from jax import lax
from jax.experimental import pallas as pl
from jax.experimental.pallas import tpu as pltpu
from jax.sharding import PartitionSpec as P

LANES = 128
SIDE = 256
MESH = pl.DeviceIdType.MESH


def ladder_kernel(
    formers, blocks, nb, depth_chunks,
    amp_ref, height_ref, owner_ref, site_ref, left_ref, right_ref, out_ref,
    left_v, right_v, sorted_v, first_panel, sums, pair_in, joined, tiles_in, amp_in, rows_out, rows_in,
    left_sem, right_sem, amp_send, amp_recv, pair_send, pair_recv,
    tile_send, tile_recv, row_send, row_recv,
):
    f = lax.axis_index("cd")
    j = lax.axis_index("ij")
    chips = formers // 2
    z = lax.div(f, 2)
    core = lax.rem(f, 2)
    devices = formers * blocks
    me = j * formers + f

    rows, depth = left_v.shape
    kc = depth // depth_chunks
    lane_tiles = right_v.shape[0] // (depth * nb)
    group = nb * lane_tiles
    per = SIDE // group
    wide = 8
    dpiece = lane_tiles * LANES
    ni, tile, _ = amp_ref.shape

    def load(k):
        return (
            pltpu.make_async_copy(
                right_ref.at[pl.ds(k * kc * group, kc * group)],
                right_v.at[pl.ds(k * kc * group, kc * group)],
                right_sem.at[k],
            ),
            pltpu.make_async_copy(
                left_ref.at[:, pl.ds(k * kc, kc)],
                left_v.at[:, pl.ds(k * kc, kc)],
                left_sem.at[k],
            ),
        )

    def remote(src, dst, send, recv, to_f, to_j):
        return pltpu.make_async_remote_copy(
            src_ref=src, dst_ref=dst, send_sem=send, recv_sem=recv,
            device_id={"cd": to_f, "ij": to_j}, device_id_type=MESH,
        )

    def amp_copy(k, landing):
        to_j = lax.rem(j + k, blocks)
        slot = j if landing is None else to_j
        columns = pl.ds(pl.multiple_of(to_j * dpiece, dpiece), dpiece)
        return remote(
            amp_ref.at[:, :, columns], amp_in.at[slot],
            amp_send.at[to_j], amp_recv.at[slot], f, to_j,
        )

    def own_amp():
        columns = pl.ds(pl.multiple_of(j * dpiece, dpiece), dpiece)
        return pltpu.make_async_copy(amp_ref.at[:, :, columns], amp_in.at[j], amp_send.at[j])

    def pair_copy(b):
        return remote(
            sums.at[b, 1 - core], pair_in.at[b], pair_send.at[b], pair_recv.at[b],
            f + 1 - 2 * core, j,
        )

    def tile_copy(b, k, landing):
        to_z = lax.rem(z + k, chips)
        slot = z if landing is None else to_z
        return remote(
            joined.at[b, to_z], tiles_in.at[b, slot],
            tile_send.at[b, to_z], tile_recv.at[b, slot], to_z * 2 + core, j,
        )

    def turned(at, step, size):
        moved = at + step
        return jnp.where(moved >= size, moved - size, moved)

    near_f = [turned(f, n, formers) for n in range(formers)]
    near_j = [turned(j, n, blocks) for n in range(blocks)]
    others = [(pf, pj) for pj in near_j for pf in near_f][1:]

    def row_copy(pf, pj):
        flat = pj * formers + pf
        return remote(rows_out.at[flat], rows_in.at[me], row_send, row_recv, pf, pj)

    for k in range(depth_chunks):
        for copy in load(k):
            copy.start()

    barrier = pltpu.get_barrier_semaphore()

    for pf, pj in others:
        pl.semaphore_signal(
            barrier, inc=1, device_id={"cd": pf, "ij": pj}, device_id_type=MESH
        )

    to = lax.broadcasted_iota(jnp.int32, (SIDE, SIDE), 0)
    origin = lax.broadcasted_iota(jnp.int32, (SIDE, SIDE), 1)
    reorder = (origin == (to % per) * group + to // per).astype(jnp.bfloat16)
    owner = owner_ref[...]
    label = ((owner & 1) * chips + (owner >> 1)) * tile + site_ref[...]
    live = lax.broadcasted_iota(jnp.int32, (1, rows), 1) < height_ref[...]
    label = jnp.where(live, label, -1)
    chosen = (
        lax.broadcasted_iota(jnp.int32, (formers * tile, rows), 0) == label
    ).astype(jnp.bfloat16)

    for k in range(depth_chunks):
        for copy in load(k):
            copy.wait()

        span = per * wide

        @pl.loop(0, kc // span, unroll=2)
        def _(m):
            base = pl.multiple_of(k * kc * group + m * (wide * SIDE), wide * SIDE)
            pieces = [right_v[pl.ds(base + w * SIDE, SIDE), :] for w in range(wide)]
            moved = jnp.dot(
                reorder, jnp.concatenate(pieces, axis=1), preferred_element_type=jnp.float32
            ).astype(jnp.bfloat16)
            first = pl.multiple_of(k * kc + m * span, span)
            for g in range(group):
                b, part = g % nb, g // nb
                column = (b % 2) * dpiece + part * LANES
                piece = moved[g * per : (g + 1) * per]
                stacked = jnp.concatenate(
                    [piece[:, w * LANES : (w + 1) * LANES] for w in range(wide)], axis=0
                )
                sorted_v[b // 2, pl.ds(first, span), column : column + LANES] = stacked

        product = jnp.dot(
            left_v[:, k * kc : (k + 1) * kc],
            sorted_v[0, k * kc : (k + 1) * kc, :],
            preferred_element_type=jnp.float32,
        )
        if k == 0:
            first_panel[...] = product
            pl.semaphore_wait(barrier, devices - 1)
            for n in range(1, blocks):
                amp_copy(n, None).start()
            own_amp().start()
        else:
            first_panel[...] = first_panel[...] + product

    def add_rows(h, panel):
        local = jnp.dot(chosen, panel.astype(jnp.bfloat16), preferred_element_type=jnp.float32)
        for b in (2 * h, 2 * h + 1):
            part = local[:, (b % 2) * dpiece : (b % 2 + 1) * dpiece]
            sums[b] = part.reshape(2, chips, tile, dpiece)
            pair_copy(b).start()

    def join(b):
        pair_copy(b).wait()
        joined[b] = sums[b, core] + pair_in[b]
        for n in range(1, chips):
            tile_copy(b, n, None).start()
        tiles_in[b, z] = joined[b, z]

    add_rows(0, first_panel[...])

    half = depth // 2
    for h in range(1, nb // 2):
        panel = jnp.dot(
            left_v[:, :half], sorted_v[h, :half, :], preferred_element_type=jnp.float32
        )
        join(2 * h - 2)
        join(2 * h - 1)
        add_rows(h, panel + jnp.dot(
            left_v[:, half:], sorted_v[h, half:, :], preferred_element_type=jnp.float32
        ))

    for n in range(1, blocks):
        amp_copy(n, True).wait()
    own_amp().wait()
    join(nb - 2)
    join(nb - 1)

    def fold(x):
        parts = [
            x[r : r + 8, c : c + LANES]
            for r in range(0, tile, 8)
            for c in range(0, dpiece, LANES)
        ]
        return functools.reduce(jnp.add, parts)

    for b in range(nb):
        for n in range(1, chips):
            tile_copy(b, n, True).wait()
        whole = tiles_in[b, 0]
        for n in range(1, chips):
            whole = whole + tiles_in[b, n]
        for s in range(blocks):
            for i in range(ni):
                rows_out[(s * ni + i) * nb + b] = jnp.sum(
                    fold(amp_in[s, i] * whole), axis=0, keepdims=True
                )

    for pf, pj in others:
        row_copy(pf, pj).start()
    rows_in[me] = rows_out[me]
    most = pl.ds(0, devices - 1)
    pltpu.make_async_copy(rows_in.at[most], rows_in.at[most], row_recv).wait()
    pltpu.make_async_copy(rows_out.at[most], rows_out.at[most], row_send).wait()

    total = rows_in[0]
    for s in range(1, devices):
        total = total + rows_in[s]
    out_ref[...] = jnp.sum(total, axis=1, keepdims=True)


def fits(left_factor, right_factor, amplitudes, formers, blocks):
    depth, nb, dpiece = right_factor.shape
    ni, tile, _ = amplitudes.shape
    if dpiece % LANES or tile % 8 or left_factor.shape[0] % 16 or formers % 2:
        return False
    group = nb * (dpiece // LANES)
    if SIDE % group or (SIDE // group) % 16 or nb % 2:
        return False
    if depth % (4 * 8 * (SIDE // group)) or ni * nb != formers:
        return False
    weights = 4 * depth * nb * dpiece + 2 * left_factor.size
    held = 4 * formers * tile * nb * dpiece * 3
    return held + weights < (40 << 20)


def by_kernel(left_factor, right_factor, amplitudes, heights, owner_map, row_site):
    formers = lax.axis_size("cd")
    blocks = lax.axis_size("ij")
    devices = formers * blocks
    chips = formers // 2
    rows, depth = left_factor.shape
    _, nb, dpiece = right_factor.shape
    ni, tile, _ = amplitudes.shape
    lane_tiles = dpiece // LANES
    chunks = 4
    flat_right = (
        right_factor.reshape(depth, nb, lane_tiles, LANES)
        .transpose(0, 2, 1, 3)
        .reshape(depth * lane_tiles * nb, LANES)
    )
    vmem = pl.BlockSpec(memory_space=pltpu.VMEM)
    hbm = pl.BlockSpec(memory_space=pl.ANY)
    dma = pltpu.SemaphoreType.DMA
    value = pl.pallas_call(
        functools.partial(ladder_kernel, formers, blocks, nb, chunks),
        out_shape=jax.ShapeDtypeStruct((1, 1), jnp.float32),
        in_specs=[hbm, vmem, vmem, vmem, hbm, hbm],
        out_specs=vmem,
        scratch_shapes=[
            pltpu.VMEM((rows, depth), jnp.bfloat16),
            pltpu.VMEM((depth * lane_tiles * nb, LANES), jnp.bfloat16),
            pltpu.VMEM((nb // 2, depth, 2 * dpiece), jnp.bfloat16),
            pltpu.VMEM((rows, 2 * dpiece), jnp.float32),
            pltpu.VMEM((nb, 2, chips, tile, dpiece), jnp.float32),
            pltpu.VMEM((nb, chips, tile, dpiece), jnp.float32),
            pltpu.VMEM((nb, chips, tile, dpiece), jnp.float32),
            pltpu.VMEM((nb, chips, tile, dpiece), jnp.float32),
            pltpu.VMEM((blocks, ni, tile, dpiece), jnp.float32),
            pltpu.VMEM((devices, 1, LANES), jnp.float32),
            pltpu.VMEM((devices, 1, LANES), jnp.float32),
            dma((chunks,)),
            dma((chunks,)),
            dma((blocks,)),
            dma((blocks,)),
            dma((nb,)),
            dma((nb,)),
            dma((nb, chips)),
            dma((nb, chips)),
            dma,
            dma,
        ],
        compiler_params=pltpu.CompilerParams(
            collective_id=0, has_side_effects=True, vmem_limit_bytes=56 << 20
        ),
    )(amplitudes, heights.reshape(1, 1), owner_map.reshape(1, rows), row_site, left_factor, flat_right)
    return value.reshape(1)


def contract(amplitudes, sums):
    return jnp.einsum("icd,cbd->ib", amplitudes, sums, precision=lax.Precision.HIGHEST)


def by_rows(left_factor, right_factor, amplitudes, heights, owner_map, row_site):
    rows = left_factor.shape[0]
    formers = lax.axis_size("cd")
    capacity = (rows + formers - 1) // formers + rows // (2 * formers)
    bwidth = right_factor.shape[1]
    dpiece = right_factor.shape[2]
    tile = amplitudes.shape[1]
    panel = jnp.dot(
        left_factor,
        right_factor.reshape(right_factor.shape[0], -1),
        preferred_element_type=jnp.float32,
    )
    position = jnp.arange(rows, dtype=jnp.int32)
    live = position < heights[0]
    panel = jnp.where(live[:, None], panel, 0.0).astype(jnp.bfloat16)
    owners = owner_map[0, :, 0]
    hits = (owners[:, None] == jnp.arange(formers, dtype=jnp.int32)[None, :]) & live[:, None]
    places = jnp.cumsum(hits.astype(jnp.int32), axis=0) - 1
    within = jnp.sum(jnp.where(hits, places, 0), axis=1)
    target = jnp.where(live, owners * capacity + within, -1)
    dispatch = jnp.arange(formers * capacity, dtype=jnp.int32)[:, None] == target[None, :]
    outgoing = jnp.dot(
        dispatch.astype(jnp.bfloat16), panel, preferred_element_type=jnp.float32
    ).astype(jnp.bfloat16)
    labels = jnp.dot(dispatch.astype(jnp.float32), row_site[0].astype(jnp.float32)).astype(
        jnp.int32
    )
    outgoing = outgoing.reshape(formers, capacity, bwidth, dpiece)
    labels = labels.reshape(formers, capacity)
    arrived, arrived_labels = (
        lax.all_to_all(outgoing, "cd", split_axis=0, concat_axis=0, tiled=True),
        lax.all_to_all(labels, "cd", split_axis=0, concat_axis=0, tiled=True),
    )
    arrived = arrived.reshape(formers * capacity, bwidth, dpiece)
    picker = (
        jnp.arange(tile, dtype=jnp.int32)[:, None] == arrived_labels.reshape(-1)[None, :]
    ).astype(jnp.bfloat16)
    whole = lax.all_gather(
        jnp.einsum("cr,rbd->cbd", picker, arrived, preferred_element_type=jnp.float32),
        "ij",
        axis=2,
        tiled=True,
    )
    partial_value = contract(amplitudes, whole)
    return lax.psum_scatter(partial_value.reshape(-1), "cd", scatter_dimension=0, tiled=True)


def on_device(left_factor, right_factor, amplitudes, heights, owner_map, row_site):
    args = (left_factor, right_factor, amplitudes, heights, owner_map, row_site)
    sizes = lax.axis_size("cd"), lax.axis_size("ij")
    if fits(left_factor, right_factor, amplitudes, *sizes):
        return by_kernel(*args)
    return by_rows(*args)


def solution(mesh):
    placed = (
        P("cd", None),
        P(None, None, "ij"),
        P("ij", "cd", None),
        P("cd"),
        P("cd", None, None),
        P("cd", None),
    )
    return jax.shard_map(
        on_device, mesh=mesh, in_specs=placed, out_specs=P(("ij", "cd")), check_vma=False
    )
```

```python
import functools

import jax
import jax.numpy as jnp
from jax import lax
from jax.experimental import pallas as pl
from jax.experimental.pallas import tpu as pltpu
from jax.sharding import PartitionSpec as P

LANES = 128
SIDE = 256
MESH = pl.DeviceIdType.MESH


def ladder_kernel(
    formers, blocks, nb, depth_chunks,
    amp_ref, height_ref, owner_ref, site_ref, left_ref, right_ref, out_ref,
    left_v, right_v, sorted_v, first_panel, sums, pair_in, joined, tiles_in, amp_in, rows_out, rows_in,
    left_sem, right_sem, amp_send, amp_recv, pair_send, pair_recv,
    tile_send, tile_recv, row_send, row_recv,
):
    f = lax.axis_index("cd")
    j = lax.axis_index("ij")
    chips = formers // 2
    z = lax.div(f, 2)
    core = lax.rem(f, 2)
    devices = formers * blocks
    me = j * formers + f

    rows, depth = left_v.shape
    kc = depth // depth_chunks
    lane_tiles = right_v.shape[0] // (depth * nb)
    group = nb * lane_tiles
    per = SIDE // group
    dpiece = lane_tiles * LANES
    ni, tile, _ = amp_ref.shape

    def load(k):
        return (
            pltpu.make_async_copy(
                right_ref.at[pl.ds(k * kc * group, kc * group)],
                right_v.at[pl.ds(k * kc * group, kc * group)],
                right_sem.at[k],
            ),
            pltpu.make_async_copy(
                left_ref.at[:, pl.ds(k * kc, kc)],
                left_v.at[:, pl.ds(k * kc, kc)],
                left_sem.at[k],
            ),
        )

    def remote(src, dst, send, recv, to_f, to_j):
        return pltpu.make_async_remote_copy(
            src_ref=src, dst_ref=dst, send_sem=send, recv_sem=recv,
            device_id={"cd": to_f, "ij": to_j}, device_id_type=MESH,
        )

    def amp_copy(k, landing):
        to_j = lax.rem(j + k, blocks)
        slot = j if landing is None else to_j
        columns = pl.ds(pl.multiple_of(to_j * dpiece, dpiece), dpiece)
        return remote(
            amp_ref.at[:, :, columns], amp_in.at[slot],
            amp_send.at[to_j], amp_recv.at[slot], f, to_j,
        )

    def pair_copy(b):
        return remote(
            sums.at[b, 1 - core], pair_in.at[b], pair_send.at[b], pair_recv.at[b],
            f + 1 - 2 * core, j,
        )

    def tile_copy(b, k, landing):
        to_z = lax.rem(z + k, chips)
        slot = z if landing is None else to_z
        return remote(
            joined.at[b, to_z], tiles_in.at[b, slot],
            tile_send.at[b, to_z], tile_recv.at[b, slot], to_z * 2 + core, j,
        )

    def turned(at, step, size):
        moved = at + step
        return jnp.where(moved >= size, moved - size, moved)

    near_f = [turned(f, n, formers) for n in range(formers)]
    near_j = [turned(j, n, blocks) for n in range(blocks)]
    others = [(pf, pj) for pj in near_j for pf in near_f][1:]

    def row_copy(pf, pj):
        flat = pj * formers + pf
        return remote(rows_out.at[flat], rows_in.at[me], row_send, row_recv, pf, pj)

    for k in range(depth_chunks):
        for copy in load(k):
            copy.start()

    barrier = pltpu.get_barrier_semaphore()

    for pf, pj in others:
        pl.semaphore_signal(
            barrier, inc=1, device_id={"cd": pf, "ij": pj}, device_id_type=MESH
        )

    to = lax.broadcasted_iota(jnp.int32, (SIDE, SIDE), 0)
    origin = lax.broadcasted_iota(jnp.int32, (SIDE, SIDE), 1)
    reorder = (origin == (to % per) * group + to // per).astype(jnp.bfloat16)
    owner = owner_ref[...]
    label = ((owner & 1) * chips + (owner >> 1)) * tile + site_ref[...]
    live = lax.broadcasted_iota(jnp.int32, (1, rows), 1) < height_ref[...]
    label = jnp.where(live, label, -1)
    chosen = (
        lax.broadcasted_iota(jnp.int32, (formers * tile, rows), 0) == label
    ).astype(jnp.bfloat16)

    for k in range(depth_chunks):
        for copy in load(k):
            copy.wait()

        @pl.loop(0, kc // (2 * per), unroll=8)
        def _(m):
            base = pl.multiple_of(k * kc * group + m * (2 * SIDE), 2 * SIDE)
            both = jnp.concatenate(
                [right_v[pl.ds(base, SIDE), :], right_v[pl.ds(base + SIDE, SIDE), :]], axis=1
            )
            moved = jnp.dot(reorder, both, preferred_element_type=jnp.float32).astype(jnp.bfloat16)
            first = pl.multiple_of(k * kc + m * (2 * per), 2 * per)
            for g in range(group):
                column = (g // nb) * LANES
                piece = moved[g * per : (g + 1) * per]
                stacked = jnp.concatenate([piece[:, :LANES], piece[:, LANES:]], axis=0)
                sorted_v[g % nb, pl.ds(first, 2 * per), column : column + LANES] = stacked

        product = jnp.dot(
            left_v[:, k * kc : (k + 1) * kc],
            sorted_v[0, k * kc : (k + 1) * kc, :],
            preferred_element_type=jnp.float32,
        )
        if k == 0:
            first_panel[...] = product
            pl.semaphore_wait(barrier, devices - 1)
            for n in range(1, blocks):
                amp_copy(n, None).start()
        else:
            first_panel[...] = first_panel[...] + product

    def add_rows(b, panel):
        local = jnp.dot(chosen, panel.astype(jnp.bfloat16), preferred_element_type=jnp.float32)
        sums[b] = local.reshape(2, chips, tile, dpiece)
        pair_copy(b).start()

    def join(b):
        pair_copy(b).wait()
        joined[b] = sums[b, core] + pair_in[b]
        for n in range(1, chips):
            tile_copy(b, n, None).start()
        tiles_in[b, z] = joined[b, z]

    add_rows(0, first_panel[...])

    @pl.loop(1, nb)
    def _(b):
        panel = jnp.dot(left_v[...], sorted_v[b], preferred_element_type=jnp.float32)
        join(b - 1)
        add_rows(b, panel)

    for n in range(1, blocks):
        amp_copy(n, True).wait()
    amp_in[j] = amp_ref[:, :, pl.ds(pl.multiple_of(j * dpiece, dpiece), dpiece)]
    join(nb - 1)

    def fold(x):
        parts = [
            x[r : r + 8, c : c + LANES]
            for r in range(0, tile, 8)
            for c in range(0, dpiece, LANES)
        ]
        return functools.reduce(jnp.add, parts)

    for b in range(nb):
        for n in range(1, chips):
            tile_copy(b, n, True).wait()
        whole = tiles_in[b, 0]
        for n in range(1, chips):
            whole = whole + tiles_in[b, n]
        for s in range(blocks):
            for i in range(ni):
                rows_out[(s * ni + i) * nb + b] = jnp.sum(
                    fold(amp_in[s, i] * whole), axis=0, keepdims=True
                )

    for pf, pj in others:
        row_copy(pf, pj).start()
    rows_in[me] = rows_out[me]
    most = pl.ds(0, devices - 1)
    pltpu.make_async_copy(rows_in.at[most], rows_in.at[most], row_recv).wait()
    pltpu.make_async_copy(rows_out.at[most], rows_out.at[most], row_send).wait()

    total = rows_in[0]
    for s in range(1, devices):
        total = total + rows_in[s]
    out_ref[...] = jnp.sum(total, axis=1, keepdims=True)


def fits(left_factor, right_factor, amplitudes, formers, blocks):
    depth, nb, dpiece = right_factor.shape
    ni, tile, _ = amplitudes.shape
    if dpiece % LANES or tile % 8 or left_factor.shape[0] % 16 or formers % 2:
        return False
    group = nb * (dpiece // LANES)
    if SIDE % group or (SIDE // group) % 16 or nb < 2:
        return False
    if depth % (4 * SIDE) or ni * nb != formers:
        return False
    weights = 4 * depth * nb * dpiece + 2 * left_factor.size
    held = 4 * formers * tile * nb * dpiece * 3
    return held + weights < (40 << 20)


def by_kernel(left_factor, right_factor, amplitudes, heights, owner_map, row_site):
    formers = lax.axis_size("cd")
    blocks = lax.axis_size("ij")
    devices = formers * blocks
    chips = formers // 2
    rows, depth = left_factor.shape
    _, nb, dpiece = right_factor.shape
    ni, tile, _ = amplitudes.shape
    lane_tiles = dpiece // LANES
    chunks = 2
    flat_right = (
        right_factor.reshape(depth, nb, lane_tiles, LANES)
        .transpose(0, 2, 1, 3)
        .reshape(depth * lane_tiles * nb, LANES)
    )
    vmem = pl.BlockSpec(memory_space=pltpu.VMEM)
    hbm = pl.BlockSpec(memory_space=pl.ANY)
    dma = pltpu.SemaphoreType.DMA
    value = pl.pallas_call(
        functools.partial(ladder_kernel, formers, blocks, nb, chunks),
        out_shape=jax.ShapeDtypeStruct((1, 1), jnp.float32),
        in_specs=[vmem, vmem, vmem, vmem, hbm, hbm],
        out_specs=vmem,
        scratch_shapes=[
            pltpu.VMEM((rows, depth), jnp.bfloat16),
            pltpu.VMEM((depth * lane_tiles * nb, LANES), jnp.bfloat16),
            pltpu.VMEM((nb, depth, dpiece), jnp.bfloat16),
            pltpu.VMEM((rows, dpiece), jnp.float32),
            pltpu.VMEM((nb, 2, chips, tile, dpiece), jnp.float32),
            pltpu.VMEM((nb, chips, tile, dpiece), jnp.float32),
            pltpu.VMEM((nb, chips, tile, dpiece), jnp.float32),
            pltpu.VMEM((nb, chips, tile, dpiece), jnp.float32),
            pltpu.VMEM((blocks, ni, tile, dpiece), jnp.float32),
            pltpu.VMEM((devices, 1, LANES), jnp.float32),
            pltpu.VMEM((devices, 1, LANES), jnp.float32),
            dma((chunks,)),
            dma((chunks,)),
            dma((blocks,)),
            dma((blocks,)),
            dma((nb,)),
            dma((nb,)),
            dma((nb, chips)),
            dma((nb, chips)),
            dma,
            dma,
        ],
        compiler_params=pltpu.CompilerParams(
            collective_id=0, has_side_effects=True, vmem_limit_bytes=56 << 20
        ),
    )(amplitudes, heights.reshape(1, 1), owner_map.reshape(1, rows), row_site, left_factor, flat_right)
    return value.reshape(1)


def contract(amplitudes, sums):
    return jnp.einsum("icd,cbd->ib", amplitudes, sums, precision=lax.Precision.HIGHEST)


def by_rows(left_factor, right_factor, amplitudes, heights, owner_map, row_site):
    rows = left_factor.shape[0]
    formers = lax.axis_size("cd")
    capacity = (rows + formers - 1) // formers + rows // (2 * formers)
    bwidth = right_factor.shape[1]
    dpiece = right_factor.shape[2]
    tile = amplitudes.shape[1]
    panel = jnp.dot(
        left_factor,
        right_factor.reshape(right_factor.shape[0], -1),
        preferred_element_type=jnp.float32,
    )
    position = jnp.arange(rows, dtype=jnp.int32)
    live = position < heights[0]
    panel = jnp.where(live[:, None], panel, 0.0).astype(jnp.bfloat16)
    owners = owner_map[0, :, 0]
    hits = (owners[:, None] == jnp.arange(formers, dtype=jnp.int32)[None, :]) & live[:, None]
    places = jnp.cumsum(hits.astype(jnp.int32), axis=0) - 1
    within = jnp.sum(jnp.where(hits, places, 0), axis=1)
    target = jnp.where(live, owners * capacity + within, -1)
    dispatch = jnp.arange(formers * capacity, dtype=jnp.int32)[:, None] == target[None, :]
    outgoing = jnp.dot(
        dispatch.astype(jnp.bfloat16), panel, preferred_element_type=jnp.float32
    ).astype(jnp.bfloat16)
    labels = jnp.dot(dispatch.astype(jnp.float32), row_site[0].astype(jnp.float32)).astype(
        jnp.int32
    )
    outgoing = outgoing.reshape(formers, capacity, bwidth, dpiece)
    labels = labels.reshape(formers, capacity)
    arrived, arrived_labels = (
        lax.all_to_all(outgoing, "cd", split_axis=0, concat_axis=0, tiled=True),
        lax.all_to_all(labels, "cd", split_axis=0, concat_axis=0, tiled=True),
    )
    arrived = arrived.reshape(formers * capacity, bwidth, dpiece)
    picker = (
        jnp.arange(tile, dtype=jnp.int32)[:, None] == arrived_labels.reshape(-1)[None, :]
    ).astype(jnp.bfloat16)
    whole = lax.all_gather(
        jnp.einsum("cr,rbd->cbd", picker, arrived, preferred_element_type=jnp.float32),
        "ij",
        axis=2,
        tiled=True,
    )
    partial_value = contract(amplitudes, whole)
    return lax.psum_scatter(partial_value.reshape(-1), "cd", scatter_dimension=0, tiled=True)


def on_device(left_factor, right_factor, amplitudes, heights, owner_map, row_site):
    args = (left_factor, right_factor, amplitudes, heights, owner_map, row_site)
    sizes = lax.axis_size("cd"), lax.axis_size("ij")
    if fits(left_factor, right_factor, amplitudes, *sizes):
        return by_kernel(*args)
    return by_rows(*args)


def solution(mesh):
    placed = (
        P("cd", None),
        P(None, None, "ij"),
        P("ij", "cd", None),
        P("cd"),
        P("cd", None, None),
        P("cd", None),
    )
    return jax.shard_map(
        on_device, mesh=mesh, in_specs=placed, out_specs=P(("ij", "cd")), check_vma=False
    )
```
